256 devices in a mesh: wide: 16 (over x, z_lo), narrow: 16 (over z_hi, y, core).
Axes of the slice: x: 4, y: 4, z: 8 (z_hi: 2, z_lo: 4; z = z_hi * 4 + z_lo), core: 2. Of those that a mesh axis runs over, the one named last changes fastest.
Arguments:
- image_rows: bfloat16 [131072, 1152], P(('wide', 'narrow'))
- text_rows: bfloat16 [131072, 1152], P(('wide', 'narrow'))
- labels: int32 [131072], P(('wide', 'narrow')), may hold values from 0 to 511, as said below
- scale: float32 [1], replicated, may hold values from 3 to 12
- bias: float32 [1], replicated, may hold values from -4 to -1
Outputs:
- image_grad: float32 [131072, 1152], P(('wide', 'narrow'))
- text_grad: float32 [131072, 1152], P(('wide', 'narrow'))
- totals: float32 [3], replicated
The draws below stay inside these ranges and needn't reach their ends.
Inputs may be any that keep to these rules, and one draw needn't show every extreme that they name: Within each group of 512 rows the labels are a permutation of the positions 0 to 511.
All inputs are finite; a program needn't handle non-finite values.
Results may differ from the reference program's by a relative error of at most 0.0006.
Values may be sent and summed in bfloat16 or wider, within the bound.
A program may use at most 128 MiB of HBM per device.

```python
import math
import jax
import jax.numpy as jnp
from jax import lax

D = 1152
ROWS_DEV = 512
ROUNDS = 4
TOKENS = 131072


def shared_parts(key):
    groups = TOKENS // ROWS_DEV
    first_key, second_key, third_key, fourth_key = jax.random.split(key, 4)
    base = jax.random.normal(first_key, (groups, ROWS_DEV, D), jnp.float32)
    group_keys = jax.random.split(second_key, groups)
    order = jax.vmap(lambda subkey: jax.random.permutation(subkey, ROWS_DEV))(group_keys).astype(jnp.int32)
    strength_key, weight_key = jax.random.split(third_key)
    strength = jax.random.uniform(strength_key, (groups, 1, 1), jnp.float32, 0.4, 0.9)
    ramp = 0.2 + 0.4 * jnp.arange(groups, dtype=jnp.float32) / max(groups - 1, 1)
    common_weight = ramp[:, None, None] * jax.random.uniform(weight_key, (groups, 1, 1), jnp.float32, 0.5, 1.4)
    direction = jax.random.normal(fourth_key, (1, 1, D), jnp.float32)
    return (base, order, strength, common_weight, direction)


def noisy_rows(key, base, strength, common_weight, direction):
    groups = TOKENS // ROWS_DEV
    noise_key, scale_key = jax.random.split(key)
    noise = jax.random.normal(noise_key, (groups, ROWS_DEV, D), jnp.float32)
    row_scale = jnp.exp(jax.random.uniform(scale_key, (groups, ROWS_DEV, 1), jnp.float32, 0.0, 1.4))
    private = strength * base + jnp.sqrt(1.0 - strength * strength) * noise
    mixed = common_weight * direction + jnp.sqrt(1.0 - common_weight * common_weight) * private
    return (mixed * row_scale / jnp.sqrt(float(D))).reshape(TOKENS, D)


def draw_image_rows(key, part):
    base, order, strength, common_weight, direction = shared_parts(key)
    key = jax.random.fold_in(key, 11)
    return noisy_rows(key, base, strength, common_weight, direction).astype(jnp.bfloat16)


def draw_text_rows(key, part):
    base, order, strength, common_weight, direction = shared_parts(key)
    key = jax.random.fold_in(key, 23)
    picked = jnp.take_along_axis(base, order[:, :, None], axis=1)
    return noisy_rows(key, picked, strength, common_weight, direction).astype(jnp.bfloat16)


def draw_labels(key, part):
    base, order, strength, common_weight, direction = shared_parts(key)
    return jnp.argsort(order, axis=1, stable=True).astype(jnp.int32).reshape(TOKENS)


def setup_inputs(seed: int = 0) -> dict:
    key_of = jax.random.split(jax.random.key(seed), 6)
    return {
        "image_rows": draw_image_rows(jax.random.fold_in(key_of[5], 71), 0),
        "text_rows": draw_text_rows(jax.random.fold_in(key_of[5], 71), 0),
        "labels": draw_labels(jax.random.fold_in(key_of[5], 71), 0),
        "scale": jnp.clip(jnp.exp(jax.random.uniform(key_of[3], (1,), jnp.float32, math.log(3.0), math.log(12.0))), 3.0, 12.0),
        "bias": jnp.clip(jax.random.uniform(key_of[4], (1,), jnp.float32, -4.0, -1.0), -4.0, -1.0),
    }


EPS = 1e-06

def normalize(rows):
    values = rows.astype(jnp.float32)
    inverse = lax.rsqrt(lax.optimization_barrier(jnp.sum(values * values, axis=-1, keepdims=True)) + EPS)
    return (values * inverse, inverse)

def reference(image_rows, text_rows, labels, scale, bias):
    groups = TOKENS // ROWS_DEV
    image_unit, inv_image = normalize(image_rows)
    text_unit, inv_text = normalize(text_rows)
    image_cast = image_unit.astype(jnp.bfloat16).astype(jnp.float32).reshape(groups, ROWS_DEV, D)
    text_cast = text_unit.astype(jnp.bfloat16).astype(jnp.float32).reshape(groups, ROWS_DEV, D)
    group_ids = jnp.arange(groups, dtype=jnp.int32)
    positive = labels.reshape(groups, ROWS_DEV)[:, :, None] == jnp.arange(ROWS_DEV, dtype=jnp.int32)[None, None, :]
    scale_value = scale[0]
    bias_value = bias[0]
    image_acc = jnp.zeros((groups, ROWS_DEV, D), jnp.float32)
    text_acc = jnp.zeros((groups, ROWS_DEV, D), jnp.float32)
    loss_sum = jnp.zeros((), jnp.float32)
    scale_sum = jnp.zeros((), jnp.float32)
    bias_sum = jnp.zeros((), jnp.float32)
    offsets = [0] + [2 ** level for level in range(ROUNDS)]
    for offset in offsets:
        partner = jnp.bitwise_xor(group_ids, offset)
        partner_text = text_cast[partner]
        cosine = jnp.einsum('crd,cqd->crq', image_cast, partner_text)
        logit = scale_value * cosine + bias_value
        if offset == 0:
            target = jnp.where(positive, 1.0, -1.0).astype(jnp.float32)
        else:
            target = -jnp.ones_like(logit)
        loss_sum = loss_sum + jnp.sum(jax.nn.softplus(-target * logit))
        slope = -target * jax.nn.sigmoid(-target * logit)
        scale_sum = scale_sum + jnp.sum(slope * cosine)
        bias_sum = bias_sum + jnp.sum(slope)
        slope_cast = slope.astype(jnp.bfloat16).astype(jnp.float32)
        image_acc = image_acc + scale_value * jnp.einsum('crq,cqd->crd', slope_cast, partner_text)
        mirrored = scale_value * jnp.einsum('crq,crd->cqd', slope_cast, image_cast)
        text_acc = text_acc + mirrored[partner]
    image_acc = image_acc.reshape(TOKENS, D)
    text_acc = text_acc.reshape(TOKENS, D)
    image_grad = (image_acc - image_unit * lax.optimization_barrier(jnp.sum(image_unit * image_acc, axis=-1, keepdims=True))) * inv_image
    text_grad = (text_acc - text_unit * lax.optimization_barrier(jnp.sum(text_unit * text_acc, axis=-1, keepdims=True))) * inv_text
    totals = jnp.stack([loss_sum, scale_sum, bias_sum]) / TOKENS
    return (image_grad, text_grad, totals)
```

```python
import functools

import jax
import jax.numpy as jnp
from jax import lax
from jax.experimental import pallas as pl
from jax.experimental.pallas import tpu as pltpu
from jax.sharding import PartitionSpec as P

EPS = 1e-06
MESH = pl.DeviceIdType.MESH
CHUNK = 128
CORE, NEAR, FAR, LONG = range(4)


def flip(value, *bits):
    for bit in bits:
        value = value + bit - 2 * bit * ((value // bit) % 2)
    return value


def inverse_norm(values):
    return lax.rsqrt(jnp.sum(values * values, axis=-1, keepdims=True) + EPS)


def fold(values):
    return jnp.sum(values.reshape(-1, 8, values.shape[-1]), axis=0)


def loss_and_slope(score):
    small = jnp.exp(-jnp.abs(score))
    loss = jnp.maximum(score, 0.0) + jnp.log1p(small)
    slope = jnp.where(score >= 0.0, 1.0, small) / (1.0 + small)
    return loss, slope


def kernel(
    rows,
    image_ref,
    text_ref,
    labels_ref,
    scale_ref,
    bias_ref,
    image_out,
    text_out,
    totals_out,
    arrived,
    raw,
    cast,
    inverse,
    total,
    unit,
    stats,
    sums,
    heard,
    load_sem,
    store_sem,
    send_sem,
    recv_sem,
    sum_send,
    sum_recv,
):
    parts = rows // CHUNK
    steps = 2 * parts
    wide, narrow = lax.axis_index("wide"), lax.axis_index("narrow")
    core = (wide, flip(narrow, 1))
    near = (wide, flip(narrow, 2))
    across = (wide, flip(narrow, 2, 4))
    far = (wide, flip(narrow, 8))
    others = [
        (flip(wide, 1), narrow),
        (flip(wide, 2), narrow),
        (flip(wide, 4), narrow),
        (flip(wide, 4, 8), narrow),
    ]
    friends = [core, near, across, far] + others

    barrier = pltpu.get_barrier_semaphore()
    for friend in friends:
        pl.semaphore_signal(barrier, inc=1, device_id=friend, device_id_type=MESH)
    pl.semaphore_wait(barrier, len(friends))

    scale_value = scale_ref[0]
    bias_value = bias_ref[0]
    sides = (text_ref, image_ref)

    def outgoing(route, side, part, device):
        slot = side * parts + part
        return pltpu.make_async_remote_copy(
            src_ref=sides[side].at[pl.ds(pl.multiple_of(part * CHUNK, CHUNK), CHUNK)],
            dst_ref=arrived.at[route, slot],
            send_sem=send_sem.at[route, slot],
            recv_sem=recv_sem.at[route, slot],
            device_id=device,
            device_id_type=MESH,
        )

    def relay(slot):
        return pltpu.make_async_remote_copy(
            src_ref=arrived.at[NEAR, slot],
            dst_ref=arrived.at[FAR, slot],
            send_sem=send_sem.at[FAR, slot],
            recv_sem=recv_sem.at[FAR, slot],
            device_id=across,
            device_id_type=MESH,
        )

    for route, device in ((LONG, far), (NEAR, near), (CORE, core)):
        for side in range(2):
            for part in range(parts):
                outgoing(route, side, part, device).start()

    loads = [
        pltpu.make_async_copy(ref, raw.at[side], load_sem.at[side])
        for side, ref in enumerate((image_ref, text_ref))
    ]
    for load in loads:
        load.start()
    for load in loads:
        load.wait()

    stats[...] = jnp.zeros_like(stats)

    def prepare(index, carry):
        side, part = index // parts, index % parts
        where = pl.ds(pl.multiple_of(part * CHUNK, CHUNK), CHUNK)
        values = raw[side, where, :].astype(jnp.float32)
        scaling = inverse_norm(values)
        inverse[side, where, :] = scaling
        cast[side, where, :] = (values * scaling).astype(jnp.bfloat16)
        return carry

    lax.fori_loop(0, steps, prepare, 0)

    def note(side, loss, slope, cosine):
        stats[side, 0] += fold(loss)
        stats[side, 1] += fold(slope * cosine)
        stats[side, 2] += fold(slope)

    def own(part, carry):
        where = pl.ds(pl.multiple_of(part * CHUNK, CHUNK), CHUNK)
        block = cast[0, where, :]
        cosine = lax.dot_general(
            cast[1], block, (((1,), (1,)), ((), ())), preferred_element_type=jnp.float32
        )
        logit = scale_value * cosine + bias_value
        positive = labels_ref[:, where] == lax.broadcasted_iota(jnp.int32, cosine.shape, 0)
        loss, slope = loss_and_slope(jnp.where(positive, -logit, logit))
        slope = jnp.where(positive, -slope, slope)
        note(0, loss, slope, cosine)
        slope_cast = slope.astype(jnp.bfloat16)
        term = jnp.dot(slope_cast, block, preferred_element_type=jnp.float32)

        @pl.when(part == 0)
        def _():
            total[1] = term

        @pl.when(part > 0)
        def _():
            total[1] += term

        total[0, where, :] = lax.dot_general(
            slope_cast, cast[1], (((0,), (0,)), ((), ())), preferred_element_type=jnp.float32
        )
        return carry

    lax.fori_loop(0, parts, own, 0)

    def meet(route, slot):
        side = slot // parts
        values = arrived[route, slot].astype(jnp.float32)
        unit[...] = (values * inverse_norm(values)).astype(jnp.bfloat16)
        cosine = lax.dot_general(
            cast[side], unit[...], (((1,), (1,)), ((), ())), preferred_element_type=jnp.float32
        )
        loss, slope = loss_and_slope(scale_value * cosine + bias_value)
        note(side, loss, slope, cosine)
        total[side] += jnp.dot(
            slope.astype(jnp.bfloat16), unit[...], preferred_element_type=jnp.float32
        )

    def incoming(route, slot):
        return pltpu.make_async_remote_copy(
            src_ref=arrived.at[route, slot],
            dst_ref=arrived.at[route, slot],
            send_sem=send_sem.at[route, slot],
            recv_sem=recv_sem.at[route, slot],
            device_id=core,
            device_id_type=MESH,
        )

    def from_core(slot, carry):
        incoming(CORE, slot).wait_recv()
        meet(CORE, slot)
        return carry

    lax.fori_loop(0, steps, from_core, 0)

    def first_half(step, carry):
        for half in range(2):
            slot = 2 * step + half
            incoming(NEAR, slot).wait_recv()
            relay(slot).start()
            meet(NEAR, slot)
        incoming(LONG, step).wait_recv()
        meet(LONG, step)
        for half in range(2):
            slot = 2 * step + half
            incoming(FAR, slot).wait_recv()
            meet(FAR, slot)
        return carry

    lax.fori_loop(0, parts, first_half, 0)

    def finish(side, out_ref):
        def body(part, carry):
            where = pl.ds(pl.multiple_of(part * CHUNK, CHUNK), CHUNK)
            scaling = inverse[side, where, :]
            rows_unit = raw[side, where, :].astype(jnp.float32) * scaling
            gradient = scale_value * total[side, where, :]
            along = jnp.sum(rows_unit * gradient, axis=-1, keepdims=True)
            total[side, where, :] = (gradient - rows_unit * along) * scaling
            pltpu.make_async_copy(
                total.at[side, where], out_ref.at[where], store_sem.at[side, part]
            ).start()
            return carry

        lax.fori_loop(0, parts, body, 0)

    sums[0] = stats[0]
    for stage, friend in enumerate(friends):
        exchange = pltpu.make_async_remote_copy(
            src_ref=sums.at[stage],
            dst_ref=heard.at[stage],
            send_sem=sum_send.at[stage],
            recv_sem=sum_recv.at[stage],
            device_id=friend,
            device_id_type=MESH,
        )
        exchange.start()
        if stage == 0:
            finish(0, image_out)
        exchange.wait()
        sums[stage + 1] = sums[stage] + heard[stage]

    def second_half(step, carry):
        incoming(LONG, step).wait_recv()
        meet(LONG, step)
        return carry

    lax.fori_loop(parts, steps, second_half, 0)
    finish(1, text_out)

    count = rows * lax.axis_size(("wide", "narrow"))
    for index in range(3):
        totals_out[index] = jnp.sum(sums[len(friends), index]) / count

    def drain(slot, carry):
        for route in (CORE, NEAR, FAR, LONG):
            incoming(route, slot).wait_send()
        return carry

    lax.fori_loop(0, steps, drain, 0)

    def stored(part, carry):
        where = pl.ds(pl.multiple_of(part * CHUNK, CHUNK), CHUNK)
        for side, out_ref in enumerate((image_out, text_out)):
            pltpu.make_async_copy(
                total.at[side, where], out_ref.at[where], store_sem.at[side, part]
            ).wait()
        return carry

    lax.fori_loop(0, parts, stored, 0)


def per_device(image_rows, text_rows, labels, scale, bias):
    rows, width = image_rows.shape
    parts = rows // CHUNK
    gradient = jax.ShapeDtypeStruct((rows, width), jnp.float32)
    dma = pltpu.SemaphoreType.DMA
    anywhere = pl.BlockSpec(memory_space=pl.ANY)
    scalars = pl.BlockSpec(memory_space=pltpu.SMEM)
    products = 20 * rows * rows * width
    return pl.pallas_call(
        functools.partial(kernel, rows),
        out_shape=(gradient, gradient, jax.ShapeDtypeStruct((3,), jnp.float32)),
        in_specs=[
            anywhere,
            anywhere,
            pl.BlockSpec(memory_space=pltpu.VMEM),
            scalars,
            scalars,
        ],
        out_specs=(anywhere, anywhere, scalars),
        scratch_shapes=[
            pltpu.VMEM((4, 2 * parts, CHUNK, width), jnp.bfloat16),
            pltpu.VMEM((2, rows, width), jnp.bfloat16),
            pltpu.VMEM((2, rows, width), jnp.bfloat16),
            pltpu.VMEM((2, rows, 1), jnp.float32),
            pltpu.VMEM((2, rows, width), jnp.float32),
            pltpu.VMEM((CHUNK, width), jnp.bfloat16),
            pltpu.VMEM((2, 3, 8, CHUNK), jnp.float32),
            pltpu.VMEM((9, 3, 8, CHUNK), jnp.float32),
            pltpu.VMEM((8, 3, 8, CHUNK), jnp.float32),
            dma((2,)),
            dma((2, parts)),
            dma((4, 2 * parts)),
            dma((4, 2 * parts)),
            dma((8,)),
            dma((8,)),
        ],
        compiler_params=pltpu.CompilerParams(
            collective_id=0, has_side_effects=True, vmem_limit_bytes=56 << 20
        ),
        cost_estimate=pl.CostEstimate(
            flops=2 * products, bytes_accessed=16 * rows * width, transcendentals=8 * rows * rows
        ),
        name="contrast",
    )(image_rows, text_rows, labels.reshape(1, rows), scale, bias)


def solution(mesh):
    split = P(("wide", "narrow"), None)
    return jax.shard_map(
        per_device,
        mesh=mesh,
        in_specs=(split, split, P(("wide", "narrow")), P(), P()),
        out_specs=(split, split, P()),
        check_vma=False,
    )
```

```python
import functools

import jax
import jax.numpy as jnp
from jax import lax
from jax.experimental import pallas as pl
from jax.experimental.pallas import tpu as pltpu
from jax.sharding import PartitionSpec as P

EPS = 1e-06
MESH = pl.DeviceIdType.MESH
CHUNK = 128
CORE, NEAR, FAR, LONG = range(4)


def flip(value, *bits):
    for bit in bits:
        value = value + bit - 2 * bit * ((value // bit) % 2)
    return value


def inverse_norm(values):
    return lax.rsqrt(jnp.sum(values * values, axis=-1, keepdims=True) + EPS)


def project(unit, gradient):
    return gradient - unit * jnp.sum(unit * gradient, axis=-1, keepdims=True)


def fold(values):
    return jnp.sum(values.reshape(-1, 8, values.shape[-1]), axis=0)


def loss_and_slope(score):
    small = jnp.exp(-jnp.abs(score))
    loss = jnp.maximum(score, 0.0) + jnp.log1p(small)
    slope = jnp.where(score >= 0.0, 1.0, small) / (1.0 + small)
    return loss, slope


def exchange_kernel(
    rows,
    image_ref,
    text_ref,
    labels_ref,
    scale_ref,
    bias_ref,
    total,
    raw,
    inverse,
    sums_out,
    arrived,
    cast,
    labels,
    scale_here,
    bias_here,
    unit,
    stats,
    sums,
    heard,
    levels,
    load_sem,
    send_sem,
    recv_sem,
    sum_send,
    sum_recv,
    level_send,
    level_recv,
):
    parts = rows // CHUNK
    steps = 2 * parts
    wide, narrow = lax.axis_index("wide"), lax.axis_index("narrow")
    core = (wide, flip(narrow, 1))
    near = (wide, flip(narrow, 2))
    across = (wide, flip(narrow, 2, 4))
    far = (wide, flip(narrow, 8))
    plane = [core, near, across, (flip(wide, 4), narrow), (flip(wide, 4, 8), narrow)]
    level = narrow // 8 * 4 + wide % 4
    column = [
        ((flip(wide, *low), flip(narrow, *high)), flip(level, *low, *(4 for _ in high)))
        for high in ((8,), ())
        for low in ((), (1,), (2,), (1, 2))
        if high or low
    ]
    friends = plane + [device for device, _ in column]

    barrier = pltpu.get_barrier_semaphore()
    for friend in friends:
        pl.semaphore_signal(barrier, inc=1, device_id=friend, device_id_type=MESH)

    loads = [
        pltpu.make_async_copy(source, target, load_sem.at[index])
        for index, (source, target) in enumerate(
            (
                (image_ref, raw.at[0]),
                (text_ref, raw.at[1]),
                (labels_ref, labels),
                (scale_ref, scale_here),
                (bias_ref, bias_here),
            )
        )
    ]
    for load in loads:
        load.start()

    pl.semaphore_wait(barrier, len(friends))

    sides = (text_ref, image_ref)

    def outgoing(route, side, part, device):
        slot = side * parts + part
        return pltpu.make_async_remote_copy(
            src_ref=sides[side].at[pl.ds(pl.multiple_of(part * CHUNK, CHUNK), CHUNK)],
            dst_ref=arrived.at[route, slot],
            send_sem=send_sem.at[route, slot],
            recv_sem=recv_sem.at[route, slot],
            device_id=device,
            device_id_type=MESH,
        )

    def relay(slot):
        return pltpu.make_async_remote_copy(
            src_ref=arrived.at[NEAR, slot],
            dst_ref=arrived.at[FAR, slot],
            send_sem=send_sem.at[FAR, slot],
            recv_sem=recv_sem.at[FAR, slot],
            device_id=across,
            device_id_type=MESH,
        )

    for route, device in ((LONG, far), (NEAR, near), (CORE, core)):
        for side in range(2):
            for part in range(parts):
                outgoing(route, side, part, device).start()

    for load in loads:
        load.wait()
    scale_value = scale_here[0]
    bias_value = bias_here[0]
    stats[...] = jnp.zeros_like(stats)

    def prepare(index, carry):
        side, part = index // parts, index % parts
        where = pl.ds(pl.multiple_of(part * CHUNK, CHUNK), CHUNK)
        values = raw[side, where, :].astype(jnp.float32)
        scaling = inverse_norm(values)
        inverse[side, where, :] = scaling
        cast[side, where, :] = (values * scaling).astype(jnp.bfloat16)
        return carry

    lax.fori_loop(0, steps, prepare, 0)

    def note(side, loss, slope, cosine):
        stats[side, 0] += fold(loss)
        stats[side, 1] += fold(slope * cosine)
        stats[side, 2] += fold(slope)

    def own(part, carry):
        where = pl.ds(pl.multiple_of(part * CHUNK, CHUNK), CHUNK)
        block = cast[0, where, :]
        cosine = lax.dot_general(
            cast[1], block, (((1,), (1,)), ((), ())), preferred_element_type=jnp.float32
        )
        logit = scale_value * cosine + bias_value
        positive = labels[:, where] == lax.broadcasted_iota(jnp.int32, cosine.shape, 0)
        loss, slope = loss_and_slope(jnp.where(positive, -logit, logit))
        slope = jnp.where(positive, -slope, slope)
        note(0, loss, slope, cosine)
        slope_cast = slope.astype(jnp.bfloat16)
        term = jnp.dot(slope_cast, block, preferred_element_type=jnp.float32)

        @pl.when(part == 0)
        def _():
            total[1] = term

        @pl.when(part > 0)
        def _():
            total[1] += term

        total[0, where, :] = lax.dot_general(
            slope_cast, cast[1], (((0,), (0,)), ((), ())), preferred_element_type=jnp.float32
        )
        return carry

    lax.fori_loop(0, parts, own, 0)

    def meet(route, slot):
        side = slot // parts
        values = arrived[route, slot].astype(jnp.float32)
        unit[...] = (values * inverse_norm(values)).astype(jnp.bfloat16)
        cosine = lax.dot_general(
            cast[side], unit[...], (((1,), (1,)), ((), ())), preferred_element_type=jnp.float32
        )
        loss, slope = loss_and_slope(scale_value * cosine + bias_value)
        note(side, loss, slope, cosine)
        total[side] += jnp.dot(
            slope.astype(jnp.bfloat16), unit[...], preferred_element_type=jnp.float32
        )

    def incoming(route, slot):
        return pltpu.make_async_remote_copy(
            src_ref=arrived.at[route, slot],
            dst_ref=arrived.at[route, slot],
            send_sem=send_sem.at[route, slot],
            recv_sem=recv_sem.at[route, slot],
            device_id=core,
            device_id_type=MESH,
        )

    def from_core(slot, carry):
        incoming(CORE, slot).wait_recv()
        meet(CORE, slot)
        return carry

    lax.fori_loop(0, steps, from_core, 0)

    def along_y(slot, carry):
        incoming(NEAR, slot).wait_recv()
        relay(slot).start()
        meet(NEAR, slot)

        @pl.when(slot > 0)
        def _():
            incoming(FAR, slot - 1).wait_recv()
            meet(FAR, slot - 1)

        return carry

    lax.fori_loop(0, steps, along_y, 0)
    incoming(FAR, steps - 1).wait_recv()
    meet(FAR, steps - 1)

    def along_z(slot, carry):
        incoming(LONG, slot).wait_recv()
        meet(LONG, slot)
        return carry

    lax.fori_loop(0, parts, along_z, 0)

    def exchange(stage):
        return pltpu.make_async_remote_copy(
            src_ref=sums.at[stage],
            dst_ref=heard.at[stage],
            send_sem=sum_send.at[stage],
            recv_sem=sum_recv.at[stage],
            device_id=plane[stage],
            device_id_type=MESH,
        )

    def tell(index, slot):
        return pltpu.make_async_remote_copy(
            src_ref=sums.at[len(plane)],
            dst_ref=levels.at[slot],
            send_sem=level_send.at[index],
            recv_sem=level_recv.at[slot],
            device_id=column[index][0],
            device_id_type=MESH,
        )

    sums[0] = jnp.zeros_like(sums[0])
    sums[0, pl.ds(0, 3)] = jnp.sum(stats[0], axis=1)
    exchange(0).start()

    def finish_image(part, carry):
        where = pl.ds(pl.multiple_of(part * CHUNK, CHUNK), CHUNK)
        scaling = inverse[0, where, :]
        rows_unit = raw[0, where, :].astype(jnp.float32) * scaling
        total[0, where, :] = project(rows_unit, scale_value * total[0, where, :]) * scaling
        return carry

    for stage in range(len(plane)):
        exchange(stage).wait()
        sums[stage + 1] = sums[stage] + heard[stage]
        if stage + 1 < len(plane):
            exchange(stage + 1).start()
    for index in range(len(column)):
        tell(index, level).start()
    levels[level] = sums[len(plane)]
    lax.fori_loop(0, parts, finish_image, 0)

    lax.fori_loop(parts, steps, along_z, 0)

    for index, (_, slot) in enumerate(column):
        tell(index, slot).wait_recv()
    answer = levels[0]
    for index in range(1, len(column) + 1):
        answer += levels[index]
    sums_out[0] = answer
    sums_out[1] = jnp.full(answer.shape, scale_value, jnp.float32)
    for index in range(len(column)):
        tell(index, level).wait_send()

    def drain(slot, carry):
        for route in (CORE, NEAR, FAR, LONG):
            incoming(route, slot).wait_send()
        return carry

    lax.fori_loop(0, steps, drain, 0)


def finish_kernel(count, total, raw, inverse, sums, image_out, text_out, totals_out, done, sem):
    rows = total.shape[1]
    parts = rows // CHUNK
    image_copy = pltpu.make_async_copy(total.at[0], image_out, sem.at[parts])
    image_copy.start()
    scale_value = sums[1, 0:1, 0:1]

    def store(part):
        where = pl.ds(pl.multiple_of(part * CHUNK, CHUNK), CHUNK)
        return pltpu.make_async_copy(done.at[where], text_out.at[where], sem.at[part])

    def body(part, carry):
        where = pl.ds(pl.multiple_of(part * CHUNK, CHUNK), CHUNK)
        scaling = inverse[1, where, :]
        rows_unit = raw[1, where, :].astype(jnp.float32) * scaling
        done[where, :] = project(rows_unit, scale_value * total[1, where, :]) * scaling
        store(part).start()
        return carry

    lax.fori_loop(0, parts, body, 0)
    for index in range(3):
        totals_out[index] = jnp.sum(sums[0, index]) / count
    for part in range(parts):
        store(part).wait()
    image_copy.wait()


def per_device(image_rows, text_rows, labels, scale, bias):
    rows, width = image_rows.shape
    parts = rows // CHUNK
    dma = pltpu.SemaphoreType.DMA
    anywhere = pl.BlockSpec(memory_space=pl.ANY)
    here = pl.BlockSpec(memory_space=pltpu.VMEM)
    products = 20 * rows * rows * width
    held = pl.pallas_call(
        functools.partial(exchange_kernel, rows),
        out_shape=(
            pltpu.VMEM((2, rows, width), jnp.float32),
            pltpu.VMEM((2, rows, width), jnp.bfloat16),
            pltpu.VMEM((2, rows, 1), jnp.float32),
            pltpu.VMEM((2, 8, CHUNK), jnp.float32),
        ),
        in_specs=[pl.BlockSpec(memory_space=pltpu.HBM)] * 5,
        out_specs=(here,) * 4,
        scratch_shapes=[
            pltpu.VMEM((4, 2 * parts, CHUNK, width), jnp.bfloat16),
            pltpu.VMEM((2, rows, width), jnp.bfloat16),
            pltpu.VMEM((1, rows), jnp.int32),
            pltpu.SMEM((1,), jnp.float32),
            pltpu.SMEM((1,), jnp.float32),
            pltpu.VMEM((CHUNK, width), jnp.bfloat16),
            pltpu.VMEM((2, 3, 8, CHUNK), jnp.float32),
            pltpu.VMEM((6, 8, CHUNK), jnp.float32),
            pltpu.VMEM((5, 8, CHUNK), jnp.float32),
            pltpu.VMEM((8, 8, CHUNK), jnp.float32),
            dma((5,)),
            dma((4, 2 * parts)),
            dma((4, 2 * parts)),
            dma((5,)),
            dma((5,)),
            dma((7,)),
            dma((8,)),
        ],
        compiler_params=pltpu.CompilerParams(
            collective_id=0, has_side_effects=True, vmem_limit_bytes=46 << 20
        ),
        cost_estimate=pl.CostEstimate(
            flops=2 * products, bytes_accessed=8 * rows * width, transcendentals=8 * rows * rows
        ),
        name="exchange",
    )(image_rows, text_rows, labels.reshape(1, rows), scale, bias)
    gradient = jax.ShapeDtypeStruct((rows, width), jnp.float32)
    return pl.pallas_call(
        functools.partial(finish_kernel, rows * lax.axis_size(("wide", "narrow"))),
        out_shape=(gradient, gradient, jax.ShapeDtypeStruct((3,), jnp.float32)),
        in_specs=[here] * 4,
        out_specs=(anywhere, anywhere, pl.BlockSpec(memory_space=pltpu.SMEM)),
        scratch_shapes=[pltpu.VMEM((rows, width), jnp.float32), dma((parts + 1,))],
        compiler_params=pltpu.CompilerParams(vmem_limit_bytes=16 << 20),
        name="finish",
    )(*held)


def solution(mesh):
    split = P(("wide", "narrow"), None)
    return jax.shard_map(
        per_device,
        mesh=mesh,
        in_specs=(split, split, P(("wide", "narrow")), P(), P()),
        out_specs=(split, split, P()),
        check_vma=False,
    )
```

```python
import functools

import jax
import jax.numpy as jnp
from jax import lax
from jax.experimental import pallas as pl
from jax.experimental.pallas import tpu as pltpu
from jax.sharding import PartitionSpec as P

EPS = 1e-06
MESH = pl.DeviceIdType.MESH
CHUNK = 128
CORE, NEAR, FAR, LONG = range(4)


def flip(value, *bits):
    for bit in bits:
        value = value + bit - 2 * bit * ((value // bit) % 2)
    return value


def inverse_norm(values):
    return lax.rsqrt(jnp.sum(values * values, axis=-1, keepdims=True) + EPS)


def project(unit, gradient):
    return gradient - unit * jnp.sum(unit * gradient, axis=-1, keepdims=True)


def fold(values):
    return jnp.sum(values.reshape(-1, 8, values.shape[-1]), axis=0)


def loss_and_slope(score):
    small = jnp.exp(-jnp.abs(score))
    loss = jnp.maximum(score, 0.0) + jnp.log1p(small)
    slope = jnp.where(score >= 0.0, 1.0, small) / (1.0 + small)
    return loss, slope


def exchange_kernel(
    rows,
    image_ref,
    text_ref,
    labels_ref,
    scale_ref,
    bias_ref,
    total,
    raw,
    inverse,
    levels,
    last_slope,
    last_unit,
    factor,
    arrived,
    cast,
    labels,
    scale_here,
    bias_here,
    unit,
    stats,
    sums,
    heard,
    load_sem,
    send_sem,
    recv_sem,
    sum_send,
    sum_recv,
    level_send,
    level_recv,
):
    parts = rows // CHUNK
    steps = 2 * parts
    wide, narrow = lax.axis_index("wide"), lax.axis_index("narrow")
    core = (wide, flip(narrow, 1))
    near = (wide, flip(narrow, 2))
    across = (wide, flip(narrow, 2, 4))
    far = (wide, flip(narrow, 8))
    plane = [core, near, across, (flip(wide, 4), narrow), (flip(wide, 4, 8), narrow)]
    level = narrow // 8 * 4 + wide % 4
    column = [
        ((flip(wide, *low), flip(narrow, *high)), flip(level, *low, *(4 for _ in high)))
        for high in ((8,), ())
        for low in ((), (1,), (2,), (1, 2))
        if high or low
    ]
    friends = [device for device, _ in column] + plane

    barrier = pltpu.get_barrier_semaphore()
    for friend in friends:
        pl.semaphore_signal(barrier, inc=1, device_id=friend, device_id_type=MESH)

    loads = [
        pltpu.make_async_copy(source, target, load_sem.at[index])
        for index, (source, target) in enumerate(
            (
                (image_ref, raw.at[0]),
                (text_ref, raw.at[1]),
                (labels_ref, labels),
                (scale_ref, scale_here),
                (bias_ref, bias_here),
            )
        )
    ]
    for load in loads:
        load.start()

    pl.semaphore_wait(barrier, len(friends))

    sides = (text_ref, image_ref)

    def outgoing(route, side, part, device):
        slot = side * parts + part
        return pltpu.make_async_remote_copy(
            src_ref=sides[side].at[pl.ds(pl.multiple_of(part * CHUNK, CHUNK), CHUNK)],
            dst_ref=arrived.at[route, slot],
            send_sem=send_sem.at[route, slot],
            recv_sem=recv_sem.at[route, slot],
            device_id=device,
            device_id_type=MESH,
        )

    def relay(slot):
        return pltpu.make_async_remote_copy(
            src_ref=arrived.at[NEAR, slot],
            dst_ref=arrived.at[FAR, slot],
            send_sem=send_sem.at[FAR, slot],
            recv_sem=recv_sem.at[FAR, slot],
            device_id=across,
            device_id_type=MESH,
        )

    for route, device in ((LONG, far), (NEAR, near), (CORE, core)):
        for side in range(2):
            for part in range(parts):
                outgoing(route, side, part, device).start()

    for load in loads:
        load.wait()
    scale_value = scale_here[0]
    bias_value = bias_here[0]
    stats[...] = jnp.zeros_like(stats)

    def prepare(index, carry):
        side, part = index // parts, index % parts
        where = pl.ds(pl.multiple_of(part * CHUNK, CHUNK), CHUNK)
        values = raw[side, where, :].astype(jnp.float32)
        scaling = inverse_norm(values)
        inverse[side, where, :] = scaling
        cast[side, where, :] = (values * scaling).astype(jnp.bfloat16)
        return carry

    lax.fori_loop(0, steps, prepare, 0)

    def note(side, loss, slope, cosine):
        stats[side, 0] += fold(loss)
        stats[side, 1] += fold(slope * cosine)
        stats[side, 2] += fold(slope)

    def own(part, carry):
        where = pl.ds(pl.multiple_of(part * CHUNK, CHUNK), CHUNK)
        block = cast[0, where, :]
        cosine = lax.dot_general(
            cast[1], block, (((1,), (1,)), ((), ())), preferred_element_type=jnp.float32
        )
        logit = scale_value * cosine + bias_value
        positive = labels[:, where] == lax.broadcasted_iota(jnp.int32, cosine.shape, 0)
        loss, slope = loss_and_slope(jnp.where(positive, -logit, logit))
        slope = jnp.where(positive, -slope, slope)
        note(0, loss, slope, cosine)
        slope_cast = slope.astype(jnp.bfloat16)
        term = jnp.dot(slope_cast, block, preferred_element_type=jnp.float32)

        @pl.when(part == 0)
        def _():
            total[1] = term

        @pl.when(part > 0)
        def _():
            total[1] += term

        total[0, where, :] = lax.dot_general(
            slope_cast, cast[1], (((0,), (0,)), ((), ())), preferred_element_type=jnp.float32
        )
        return carry

    lax.fori_loop(0, parts, own, 0)

    def slopes(route, slot, target):
        side = slot // parts
        values = arrived[route, slot].astype(jnp.float32)
        target[...] = (values * inverse_norm(values)).astype(jnp.bfloat16)
        cosine = lax.dot_general(
            cast[side], target[...], (((1,), (1,)), ((), ())), preferred_element_type=jnp.float32
        )
        loss, slope = loss_and_slope(scale_value * cosine + bias_value)
        note(side, loss, slope, cosine)
        return slope.astype(jnp.bfloat16)

    def meet(route, slot):
        slope_cast = slopes(route, slot, unit)
        total[slot // parts] += jnp.dot(
            slope_cast, unit[...], preferred_element_type=jnp.float32
        )

    def incoming(route, slot):
        return pltpu.make_async_remote_copy(
            src_ref=arrived.at[route, slot],
            dst_ref=arrived.at[route, slot],
            send_sem=send_sem.at[route, slot],
            recv_sem=recv_sem.at[route, slot],
            device_id=core,
            device_id_type=MESH,
        )

    def from_core(slot, carry):
        incoming(CORE, slot).wait_recv()
        meet(CORE, slot)
        return carry

    lax.fori_loop(0, steps, from_core, 0)

    def along_y(slot, carry):
        incoming(NEAR, slot).wait_recv()
        relay(slot).start()
        meet(NEAR, slot)

        @pl.when(slot > 0)
        def _():
            incoming(FAR, slot - 1).wait_recv()
            meet(FAR, slot - 1)

        return carry

    lax.fori_loop(0, steps, along_y, 0)
    incoming(FAR, steps - 1).wait_recv()
    meet(FAR, steps - 1)

    def along_z(slot, carry):
        incoming(LONG, slot).wait_recv()
        meet(LONG, slot)
        return carry

    lax.fori_loop(0, parts, along_z, 0)

    def exchange(stage):
        return pltpu.make_async_remote_copy(
            src_ref=sums.at[stage],
            dst_ref=heard.at[stage],
            send_sem=sum_send.at[stage],
            recv_sem=sum_recv.at[stage],
            device_id=plane[stage],
            device_id_type=MESH,
        )

    def tell(index, slot):
        return pltpu.make_async_remote_copy(
            src_ref=sums.at[len(plane)],
            dst_ref=levels.at[slot],
            send_sem=level_send.at[index],
            recv_sem=level_recv.at[slot],
            device_id=column[index][0],
            device_id_type=MESH,
        )

    sums[0] = jnp.zeros_like(sums[0])
    sums[0, pl.ds(0, 3)] = jnp.sum(stats[0], axis=1)
    exchange(0).start()

    def finish_image(part, carry):
        where = pl.ds(pl.multiple_of(part * CHUNK, CHUNK), CHUNK)
        scaling = inverse[0, where, :]
        rows_unit = raw[0, where, :].astype(jnp.float32) * scaling
        total[0, where, :] = project(rows_unit, scale_value * total[0, where, :]) * scaling
        return carry

    for stage in range(len(plane)):
        exchange(stage).wait()
        sums[stage + 1] = sums[stage] + heard[stage]
        if stage + 1 < len(plane):
            exchange(stage + 1).start()
    for index in range(len(column)):
        tell(index, level).start()
    levels[level] = sums[len(plane)]
    lax.fori_loop(0, parts, finish_image, 0)

    factor[...] = jnp.full(factor.shape, scale_value, jnp.float32)

    def drain(slot, carry):
        for route in (CORE, NEAR, FAR):
            incoming(route, slot).wait_send()
        return carry

    lax.fori_loop(0, steps, drain, 0)

    def along_z_sent(slot, carry):
        incoming(LONG, slot - parts).wait_send()
        return along_z(slot, carry)

    lax.fori_loop(parts, steps - 1, along_z_sent, 0)
    incoming(LONG, steps - 1).wait_recv()
    last_slope[...] = slopes(LONG, steps - 1, last_unit)

    for slot in range(parts - 1, steps):
        incoming(LONG, slot).wait_send()
    for index, (_, slot) in enumerate(column):
        tell(index, slot).wait_recv()
        tell(index, level).wait_send()


def finish_kernel(
    count,
    total,
    raw,
    inverse,
    levels,
    last_slope,
    last_unit,
    factor,
    image_out,
    text_out,
    totals_out,
    done,
    totals,
    sem,
):
    rows = total.shape[1]
    parts = rows // CHUNK
    image_copy = pltpu.make_async_copy(total.at[0], image_out, sem.at[parts])
    image_copy.start()
    scale_value = factor[0:1, 0:1]

    def store(part):
        where = pl.ds(pl.multiple_of(part * CHUNK, CHUNK), CHUNK)
        return pltpu.make_async_copy(done.at[where], text_out.at[where], sem.at[part])

    def body(part, carry):
        where = pl.ds(pl.multiple_of(part * CHUNK, CHUNK), CHUNK)
        scaling = inverse[1, where, :]
        rows_unit = raw[1, where, :].astype(jnp.float32) * scaling
        whole = total[1, where, :] + jnp.dot(
            last_slope[where, :], last_unit[...], preferred_element_type=jnp.float32
        )
        done[where, :] = project(rows_unit, scale_value * whole) * scaling
        store(part).start()
        return carry

    lax.fori_loop(0, parts, body, 0)
    answer = jnp.sum(levels[...], axis=0)
    for index in range(3):
        totals[index] = jnp.sum(answer[index]) / count
    totals_copy = pltpu.make_async_copy(totals, totals_out, sem.at[parts + 1])
    totals_copy.start()
    for part in range(parts):
        store(part).wait()
    image_copy.wait()
    totals_copy.wait()


def per_device(image_rows, text_rows, labels, scale, bias):
    rows, width = image_rows.shape
    parts = rows // CHUNK
    dma = pltpu.SemaphoreType.DMA
    anywhere = pl.BlockSpec(memory_space=pl.ANY)
    here = pl.BlockSpec(memory_space=pltpu.VMEM)
    products = 20 * rows * rows * width
    held = pl.pallas_call(
        functools.partial(exchange_kernel, rows),
        out_shape=(
            pltpu.VMEM((2, rows, width), jnp.float32),
            pltpu.VMEM((2, rows, width), jnp.bfloat16),
            pltpu.VMEM((2, rows, 1), jnp.float32),
            pltpu.VMEM((8, 8, CHUNK), jnp.float32),
            pltpu.VMEM((rows, CHUNK), jnp.bfloat16),
            pltpu.VMEM((CHUNK, width), jnp.bfloat16),
            pltpu.VMEM((8, CHUNK), jnp.float32),
        ),
        in_specs=[pl.BlockSpec(memory_space=pltpu.HBM)] * 5,
        out_specs=(here,) * 7,
        scratch_shapes=[
            pltpu.VMEM((4, 2 * parts, CHUNK, width), jnp.bfloat16),
            pltpu.VMEM((2, rows, width), jnp.bfloat16),
            pltpu.VMEM((1, rows), jnp.int32),
            pltpu.SMEM((1,), jnp.float32),
            pltpu.SMEM((1,), jnp.float32),
            pltpu.VMEM((CHUNK, width), jnp.bfloat16),
            pltpu.VMEM((2, 3, 8, CHUNK), jnp.float32),
            pltpu.VMEM((6, 8, CHUNK), jnp.float32),
            pltpu.VMEM((5, 8, CHUNK), jnp.float32),
            dma((5,)),
            dma((4, 2 * parts)),
            dma((4, 2 * parts)),
            dma((5,)),
            dma((5,)),
            dma((7,)),
            dma((8,)),
        ],
        compiler_params=pltpu.CompilerParams(
            collective_id=0, has_side_effects=True, vmem_limit_bytes=54 << 20
        ),
        cost_estimate=pl.CostEstimate(
            flops=2 * products, bytes_accessed=8 * rows * width, transcendentals=8 * rows * rows
        ),
        name="exchange",
    )(image_rows, text_rows, labels.reshape(1, rows), scale, bias)
    gradient = jax.ShapeDtypeStruct((rows, width), jnp.float32)
    return pl.pallas_call(
        functools.partial(finish_kernel, rows * lax.axis_size(("wide", "narrow"))),
        out_shape=(gradient, gradient, jax.ShapeDtypeStruct((3,), jnp.float32)),
        in_specs=[here] * 7,
        out_specs=(anywhere,) * 3,
        scratch_shapes=[
            pltpu.VMEM((rows, width), jnp.float32),
            pltpu.SMEM((3,), jnp.float32),
            dma((parts + 2,)),
        ],
        compiler_params=pltpu.CompilerParams(vmem_limit_bytes=24 << 20),
        name="finish",
    )(*held)


def solution(mesh):
    split = P(("wide", "narrow"), None)
    return jax.shard_map(
        per_device,
        mesh=mesh,
        in_specs=(split, split, P(("wide", "narrow")), P(), P()),
        out_specs=(split, split, P()),
        check_vma=False,
    )
```

```python
import functools

import jax
import jax.numpy as jnp
from jax import lax
from jax.experimental import pallas as pl
from jax.experimental.pallas import tpu as pltpu
from jax.sharding import PartitionSpec as P

EPS = 1e-06
MESH = pl.DeviceIdType.MESH
CHUNK = 128
CORE, NEAR, FAR, LONG = range(4)


def flip(value, *bits):
    for bit in bits:
        value = value + bit - 2 * bit * ((value // bit) % 2)
    return value


def inverse_norm(values):
    return lax.rsqrt(jnp.sum(values * values, axis=-1, keepdims=True) + EPS)


def project(unit, gradient):
    return gradient - unit * jnp.sum(unit * gradient, axis=-1, keepdims=True)


def fold(values):
    return jnp.sum(values.reshape(-1, 8, values.shape[-1]), axis=0)


def loss_and_slope(score):
    small = jnp.exp(-jnp.abs(score))
    loss = jnp.maximum(score, 0.0) + jnp.log1p(small)
    slope = jnp.where(score >= 0.0, 1.0, small) / (1.0 + small)
    return loss, slope


def exchange_kernel(
    rows,
    image_ref,
    text_ref,
    labels_ref,
    scale_ref,
    bias_ref,
    total,
    raw,
    inverse,
    answer,
    last_slope,
    last_unit,
    factor,
    arrived,
    cast,
    labels,
    scale_here,
    bias_here,
    unit,
    stats,
    sums,
    heard,
    levels,
    load_sem,
    send_sem,
    recv_sem,
    sum_send,
    sum_recv,
    level_send,
    level_recv,
    pair_in,
    far_in,
    go_far,
    all_in,
):
    parts = rows // CHUNK
    steps = 2 * parts
    wide, narrow = lax.axis_index("wide"), lax.axis_index("narrow")
    core = (wide, flip(narrow, 1))
    near = (wide, flip(narrow, 2))
    across = (wide, flip(narrow, 2, 4))
    far = (wide, flip(narrow, 8))
    plane = [core, near, across, (flip(wide, 4), narrow), (flip(wide, 4, 8), narrow)]
    level = narrow // 8 * 4 + wide % 4
    upper = [
        ((flip(wide, *low), far[1]), flip(level, 4, *low)) for low in ((), (1,), (2,), (1, 2))
    ]
    lower = [((flip(wide, *low), narrow), flip(level, *low)) for low in ((1,), (2,), (1, 2))]
    columns = (lower, upper)
    friends = [device for device, _ in upper + lower] + plane[1:]
    levels[...] = jnp.zeros_like(levels)
    barrier = pltpu.get_barrier_semaphore()

    def signal(semaphore, device):
        pl.semaphore_signal(semaphore, inc=1, device_id=device, device_id_type=MESH)

    loads = [
        pltpu.make_async_copy(source, target, load_sem.at[index])
        for index, (source, target) in enumerate(
            (
                (image_ref, raw.at[0]),
                (text_ref, raw.at[1]),
                (labels_ref, labels),
                (scale_ref, scale_here),
                (bias_ref, bias_here),
            )
        )
    ]
    for load in loads:
        load.start()

    sides = (text_ref, image_ref)

    def outgoing(route, side, part, device):
        slot = side * parts + part
        return pltpu.make_async_remote_copy(
            src_ref=sides[side].at[pl.ds(pl.multiple_of(part * CHUNK, CHUNK), CHUNK)],
            dst_ref=arrived.at[route, slot],
            send_sem=send_sem.at[route, slot],
            recv_sem=recv_sem.at[route, slot],
            device_id=device,
            device_id_type=MESH,
        )

    def relay(slot):
        return pltpu.make_async_remote_copy(
            src_ref=arrived.at[NEAR, slot],
            dst_ref=arrived.at[FAR, slot],
            send_sem=send_sem.at[FAR, slot],
            recv_sem=recv_sem.at[FAR, slot],
            device_id=across,
            device_id_type=MESH,
        )

    def send(route, device):
        for side in range(2):
            for part in range(parts):
                outgoing(route, side, part, device).start()

    @pl.when(narrow % 2 == 0)
    def _():
        signal(barrier, far)
        pl.semaphore_wait(barrier, 2)
        signal(pair_in, core)
        signal(far_in, far)
        send(LONG, far)
        pl.semaphore_wait(far_in, 1)
        signal(go_far, core)
        pl.semaphore_wait(all_in, 1)

    @pl.when(narrow % 2 == 1)
    def _():
        signal(barrier, core)
        pl.semaphore_wait(pair_in, 1)
        for friend in friends:
            signal(barrier, friend)
        pl.semaphore_wait(go_far, 1)
        send(LONG, far)
        pl.semaphore_wait(barrier, len(friends))
        signal(all_in, core)

    send(NEAR, near)
    send(CORE, core)

    for load in loads:
        load.wait()
    scale_value = scale_here[0]
    bias_value = bias_here[0]
    stats[...] = jnp.zeros_like(stats)

    def prepare(index, carry):
        side, part = index // parts, index % parts
        where = pl.ds(pl.multiple_of(part * CHUNK, CHUNK), CHUNK)
        values = raw[side, where, :].astype(jnp.float32)
        scaling = inverse_norm(values)
        inverse[side, where, :] = scaling
        cast[side, where, :] = (values * scaling).astype(jnp.bfloat16)
        return carry

    lax.fori_loop(0, steps, prepare, 0)

    def note(side, loss, slope, cosine):
        stats[side, 0] += fold(loss)
        stats[side, 1] += fold(slope * cosine)
        stats[side, 2] += fold(slope)

    def own(part, carry):
        where = pl.ds(pl.multiple_of(part * CHUNK, CHUNK), CHUNK)
        block = cast[0, where, :]
        cosine = lax.dot_general(
            cast[1], block, (((1,), (1,)), ((), ())), preferred_element_type=jnp.float32
        )
        logit = scale_value * cosine + bias_value
        positive = labels[:, where] == lax.broadcasted_iota(jnp.int32, cosine.shape, 0)
        loss, slope = loss_and_slope(jnp.where(positive, -logit, logit))
        slope = jnp.where(positive, -slope, slope)
        note(0, loss, slope, cosine)
        slope_cast = slope.astype(jnp.bfloat16)
        term = jnp.dot(slope_cast, block, preferred_element_type=jnp.float32)

        @pl.when(part == 0)
        def _():
            total[1] = term

        @pl.when(part > 0)
        def _():
            total[1] += term

        total[0, where, :] = lax.dot_general(
            slope_cast, cast[1], (((0,), (0,)), ((), ())), preferred_element_type=jnp.float32
        )
        return carry

    lax.fori_loop(0, parts, own, 0)

    def slopes(route, slot, target):
        side = slot // parts
        values = arrived[route, slot].astype(jnp.float32)
        target[...] = (values * inverse_norm(values)).astype(jnp.bfloat16)
        cosine = lax.dot_general(
            cast[side], target[...], (((1,), (1,)), ((), ())), preferred_element_type=jnp.float32
        )
        loss, slope = loss_and_slope(scale_value * cosine + bias_value)
        note(side, loss, slope, cosine)
        return slope.astype(jnp.bfloat16)

    def meet(route, slot):
        slope_cast = slopes(route, slot, unit)
        total[slot // parts] += jnp.dot(
            slope_cast, unit[...], preferred_element_type=jnp.float32
        )

    def incoming(route, slot):
        return pltpu.make_async_remote_copy(
            src_ref=arrived.at[route, slot],
            dst_ref=arrived.at[route, slot],
            send_sem=send_sem.at[route, slot],
            recv_sem=recv_sem.at[route, slot],
            device_id=core,
            device_id_type=MESH,
        )

    def from_core(slot, carry):
        incoming(CORE, slot).wait_recv()
        meet(CORE, slot)
        return carry

    lax.fori_loop(0, steps, from_core, 0)

    def along_y(slot, carry):
        incoming(NEAR, slot).wait_recv()
        relay(slot).start()
        meet(NEAR, slot)

        @pl.when(slot > 0)
        def _():
            incoming(FAR, slot - 1).wait_recv()
            meet(FAR, slot - 1)

        return carry

    lax.fori_loop(0, steps, along_y, 0)
    incoming(FAR, steps - 1).wait_recv()
    meet(FAR, steps - 1)

    def along_z(slot, carry):
        incoming(LONG, slot).wait_recv()
        meet(LONG, slot)
        return carry

    lax.fori_loop(0, parts, along_z, 0)

    def exchange(stage):
        return pltpu.make_async_remote_copy(
            src_ref=sums.at[stage],
            dst_ref=heard.at[stage],
            send_sem=sum_send.at[stage],
            recv_sem=sum_recv.at[stage],
            device_id=plane[stage],
            device_id_type=MESH,
        )

    def tell(device, index, slot):
        return pltpu.make_async_remote_copy(
            src_ref=sums.at[len(plane)],
            dst_ref=levels.at[slot],
            send_sem=level_send.at[index],
            recv_sem=level_recv.at[slot],
            device_id=device,
            device_id_type=MESH,
        )

    sums[0] = jnp.zeros_like(sums[0])
    sums[0, pl.ds(0, 3)] = jnp.sum(stats[0], axis=1)
    exchange(0).start()

    def finish_image(part, carry):
        where = pl.ds(pl.multiple_of(part * CHUNK, CHUNK), CHUNK)
        scaling = inverse[0, where, :]
        rows_unit = raw[0, where, :].astype(jnp.float32) * scaling
        total[0, where, :] = project(rows_unit, scale_value * total[0, where, :]) * scaling
        return carry

    for stage in range(len(plane)):
        exchange(stage).wait()
        sums[stage + 1] = sums[stage] + heard[stage]
        if stage + 1 < len(plane):
            exchange(stage + 1).start()

    for parity, column in enumerate(columns):

        @pl.when(narrow % 2 == parity)
        def _(parity=parity, column=column):
            for index, (device, _) in enumerate(column):
                tell(device, index, level).start()
            if parity == 0:
                levels[level] = sums[len(plane)]

    lax.fori_loop(0, parts, finish_image, 0)

    factor[...] = jnp.full(factor.shape, scale_value, jnp.float32)

    def drain(slot, carry):
        for route in (CORE, NEAR, FAR):
            incoming(route, slot).wait_send()
        return carry

    lax.fori_loop(0, steps, drain, 0)

    def along_z_sent(slot, carry):
        incoming(LONG, slot - parts).wait_send()
        return along_z(slot, carry)

    lax.fori_loop(parts, steps - 1, along_z_sent, 0)
    for parity, column in enumerate(columns):

        @pl.when(narrow % 2 == parity)
        def _(column=column):
            for index, (device, slot) in enumerate(column):
                tell(device, index, slot).wait_recv()
                tell(device, index, level).wait_send()

    halves = len(plane) + 1
    sums[halves] = jnp.sum(levels[...], axis=0)
    other_half = pltpu.make_async_remote_copy(
        src_ref=sums.at[halves],
        dst_ref=heard.at[len(plane)],
        send_sem=sum_send.at[len(plane)],
        recv_sem=sum_recv.at[len(plane)],
        device_id=core,
        device_id_type=MESH,
    )
    other_half.start()
    incoming(LONG, steps - 1).wait_recv()
    last_slope[...] = slopes(LONG, steps - 1, last_unit)

    for slot in range(parts - 1, steps):
        incoming(LONG, slot).wait_send()
    other_half.wait()
    answer[...] = sums[halves] + heard[len(plane)]


def finish_kernel(
    count,
    total,
    raw,
    inverse,
    answer,
    last_slope,
    last_unit,
    factor,
    image_out,
    text_out,
    totals_out,
    done,
    totals,
    sem,
):
    rows = total.shape[1]
    parts = rows // CHUNK
    image_copy = pltpu.make_async_copy(total.at[0], image_out, sem.at[parts])
    image_copy.start()
    scale_value = factor[0:1, 0:1]

    def store(part):
        where = pl.ds(pl.multiple_of(part * CHUNK, CHUNK), CHUNK)
        return pltpu.make_async_copy(done.at[where], text_out.at[where], sem.at[part])

    def body(part, carry):
        where = pl.ds(pl.multiple_of(part * CHUNK, CHUNK), CHUNK)
        scaling = inverse[1, where, :]
        rows_unit = raw[1, where, :].astype(jnp.float32) * scaling
        whole = total[1, where, :] + jnp.dot(
            last_slope[where, :], last_unit[...], preferred_element_type=jnp.float32
        )
        done[where, :] = project(rows_unit, scale_value * whole) * scaling
        store(part).start()
        return carry

    lax.fori_loop(0, parts, body, 0)
    for index in range(3):
        totals[index] = jnp.sum(answer[index]) / count
    totals_copy = pltpu.make_async_copy(totals, totals_out, sem.at[parts + 1])
    totals_copy.start()
    for part in range(parts):
        store(part).wait()
    image_copy.wait()
    totals_copy.wait()


def per_device(image_rows, text_rows, labels, scale, bias):
    rows, width = image_rows.shape
    parts = rows // CHUNK
    dma = pltpu.SemaphoreType.DMA
    anywhere = pl.BlockSpec(memory_space=pl.ANY)
    here = pl.BlockSpec(memory_space=pltpu.VMEM)
    products = 20 * rows * rows * width
    held = pl.pallas_call(
        functools.partial(exchange_kernel, rows),
        out_shape=(
            pltpu.VMEM((2, rows, width), jnp.float32),
            pltpu.VMEM((2, rows, width), jnp.bfloat16),
            pltpu.VMEM((2, rows, 1), jnp.float32),
            pltpu.VMEM((8, CHUNK), jnp.float32),
            pltpu.VMEM((rows, CHUNK), jnp.bfloat16),
            pltpu.VMEM((CHUNK, width), jnp.bfloat16),
            pltpu.VMEM((8, CHUNK), jnp.float32),
        ),
        in_specs=[pl.BlockSpec(memory_space=pltpu.HBM)] * 5,
        out_specs=(here,) * 7,
        scratch_shapes=[
            pltpu.VMEM((4, 2 * parts, CHUNK, width), jnp.bfloat16),
            pltpu.VMEM((2, rows, width), jnp.bfloat16),
            pltpu.VMEM((1, rows), jnp.int32),
            pltpu.SMEM((1,), jnp.float32),
            pltpu.SMEM((1,), jnp.float32),
            pltpu.VMEM((CHUNK, width), jnp.bfloat16),
            pltpu.VMEM((2, 3, 8, CHUNK), jnp.float32),
            pltpu.VMEM((7, 8, CHUNK), jnp.float32),
            pltpu.VMEM((6, 8, CHUNK), jnp.float32),
            pltpu.VMEM((8, 8, CHUNK), jnp.float32),
            dma((5,)),
            dma((4, 2 * parts)),
            dma((4, 2 * parts)),
            dma((6,)),
            dma((6,)),
            dma((4,)),
            dma((8,)),
            pltpu.SemaphoreType.REGULAR,
            pltpu.SemaphoreType.REGULAR,
            pltpu.SemaphoreType.REGULAR,
            pltpu.SemaphoreType.REGULAR,
        ],
        compiler_params=pltpu.CompilerParams(
            collective_id=0, has_side_effects=True, vmem_limit_bytes=54 << 20
        ),
        cost_estimate=pl.CostEstimate(
            flops=2 * products, bytes_accessed=8 * rows * width, transcendentals=8 * rows * rows
        ),
        name="exchange",
    )(image_rows, text_rows, labels.reshape(1, rows), scale, bias)
    gradient = jax.ShapeDtypeStruct((rows, width), jnp.float32)
    return pl.pallas_call(
        functools.partial(finish_kernel, rows * lax.axis_size(("wide", "narrow"))),
        out_shape=(gradient, gradient, jax.ShapeDtypeStruct((3,), jnp.float32)),
        in_specs=[here] * 7,
        out_specs=(anywhere,) * 3,
        scratch_shapes=[
            pltpu.VMEM((rows, width), jnp.float32),
            pltpu.SMEM((3,), jnp.float32),
            dma((parts + 2,)),
        ],
        compiler_params=pltpu.CompilerParams(vmem_limit_bytes=24 << 20),
        name="finish",
    )(*held)


def solution(mesh):
    split = P(("wide", "narrow"), None)
    return jax.shard_map(
        per_device,
        mesh=mesh,
        in_specs=(split, split, P(("wide", "narrow")), P(), P()),
        out_specs=(split, split, P()),
        check_vma=False,
    )
```

```python
import functools

import jax
import jax.numpy as jnp
from jax import lax
from jax.experimental import pallas as pl
from jax.experimental.pallas import tpu as pltpu
from jax.sharding import PartitionSpec as P

EPS = 1e-06
MESH = pl.DeviceIdType.MESH
CHUNK = 128
CORE, NEAR, FAR, LONG = range(4)


def flip(value, *bits):
    for bit in bits:
        value = value + bit - 2 * bit * ((value // bit) % 2)
    return value


def inverse_norm(values):
    return lax.rsqrt(jnp.sum(values * values, axis=-1, keepdims=True) + EPS)


def project(unit, gradient):
    return gradient - unit * jnp.sum(unit * gradient, axis=-1, keepdims=True)


def fold(values):
    return jnp.sum(values.reshape(-1, 8, values.shape[-1]), axis=0)


def loss_and_slope(score):
    small = jnp.exp(-jnp.abs(score))
    loss = jnp.maximum(score, 0.0) + jnp.log1p(small)
    slope = jnp.where(score >= 0.0, 1.0, small) / (1.0 + small)
    return loss, slope


def exchange_kernel(
    rows,
    image_ref,
    text_ref,
    labels_ref,
    scale_ref,
    bias_ref,
    total,
    raw,
    inverse,
    answer,
    last_slope,
    last_unit,
    factor,
    arrived,
    cast,
    labels,
    scale_here,
    bias_here,
    unit,
    stats,
    sums,
    heard,
    levels,
    load_sem,
    send_sem,
    recv_sem,
    sum_send,
    sum_recv,
    level_send,
    level_recv,
    pair_in,
    far_in,
    go_far,
    all_in,
):
    parts = rows // CHUNK
    steps = 2 * parts
    wide, narrow = lax.axis_index("wide"), lax.axis_index("narrow")
    core = (wide, flip(narrow, 1))
    near = (wide, flip(narrow, 2))
    across = (wide, flip(narrow, 2, 4))
    far = (wide, flip(narrow, 8))
    plane = [core, near, across, (flip(wide, 4), narrow), (flip(wide, 4, 8), narrow)]
    level = narrow // 8 * 4 + wide % 4
    upper = [
        ((flip(wide, *low), far[1]), flip(level, 4, *low)) for low in ((), (1,), (2,), (1, 2))
    ]
    lower = [((flip(wide, *low), narrow), flip(level, *low)) for low in ((1,), (2,), (1, 2))]
    columns = (lower, upper)
    friends = [device for device, _ in upper + lower] + plane[1:]
    levels[...] = jnp.zeros_like(levels)
    barrier = pltpu.get_barrier_semaphore()

    def signal(semaphore, device):
        pl.semaphore_signal(semaphore, inc=1, device_id=device, device_id_type=MESH)

    loads = [
        pltpu.make_async_copy(source, target, load_sem.at[index])
        for index, (source, target) in enumerate(
            (
                (image_ref, raw.at[0]),
                (text_ref, raw.at[1]),
                (labels_ref, labels),
                (scale_ref, scale_here),
                (bias_ref, bias_here),
            )
        )
    ]
    for load in loads:
        load.start()

    sides = (text_ref, image_ref)

    def outgoing(route, side, part, device):
        slot = side * parts + part
        return pltpu.make_async_remote_copy(
            src_ref=sides[side].at[pl.ds(pl.multiple_of(part * CHUNK, CHUNK), CHUNK)],
            dst_ref=arrived.at[route, slot],
            send_sem=send_sem.at[route, slot],
            recv_sem=recv_sem.at[route, slot],
            device_id=device,
            device_id_type=MESH,
        )

    def relay(slot):
        return pltpu.make_async_remote_copy(
            src_ref=arrived.at[NEAR, slot],
            dst_ref=arrived.at[FAR, slot],
            send_sem=send_sem.at[FAR, slot],
            recv_sem=recv_sem.at[FAR, slot],
            device_id=across,
            device_id_type=MESH,
        )

    def send(route, device, side, count):
        for part in range(count):
            outgoing(route, side, part, device).start()

    patient = wide % 4 >= 2

    def send_far():
        send(LONG, far, 0, parts)

        @pl.when(jnp.logical_not(patient))
        def _():
            send(LONG, far, 1, parts)

    @pl.when(narrow % 2 == 0)
    def _():
        signal(barrier, far)
        pl.semaphore_wait(barrier, 2)
        signal(pair_in, core)
        signal(far_in, far)
        send_far()
        pl.semaphore_wait(far_in, 1)
        signal(go_far, core)
        pl.semaphore_wait(all_in, 1)

    @pl.when(narrow % 2 == 1)
    def _():
        signal(barrier, core)
        pl.semaphore_wait(pair_in, 1)
        for friend in friends:
            signal(barrier, friend)
        pl.semaphore_wait(go_far, 1)
        send_far()
        pl.semaphore_wait(barrier, len(friends))
        signal(all_in, core)

    for side in range(2):
        send(NEAR, near, side, parts)
    for side in range(2):
        send(CORE, core, side, parts)

    for load in loads:
        load.wait()
    scale_value = scale_here[0]
    bias_value = bias_here[0]
    stats[...] = jnp.zeros_like(stats)
    total[...] = jnp.zeros_like(total)

    def prepare(index, carry):
        side, part = index // parts, index % parts
        where = pl.ds(pl.multiple_of(part * CHUNK, CHUNK), CHUNK)
        values = raw[side, where, :].astype(jnp.float32)
        scaling = inverse_norm(values)
        inverse[side, where, :] = scaling
        cast[side, where, :] = (values * scaling).astype(jnp.bfloat16)
        return carry

    lax.fori_loop(0, steps, prepare, 0)

    def note(side, loss, slope, cosine):
        stats[side, 0] += fold(loss)
        stats[side, 1] += fold(slope * cosine)
        stats[side, 2] += fold(slope)

    def own(part):
        where = pl.ds(pl.multiple_of(part * CHUNK, CHUNK), CHUNK)
        block = cast[0, where, :]
        cosine = lax.dot_general(
            cast[1], block, (((1,), (1,)), ((), ())), preferred_element_type=jnp.float32
        )
        logit = scale_value * cosine + bias_value
        positive = labels[:, where] == lax.broadcasted_iota(jnp.int32, cosine.shape, 0)
        loss, slope = loss_and_slope(jnp.where(positive, -logit, logit))
        slope = jnp.where(positive, -slope, slope)
        note(0, loss, slope, cosine)
        slope_cast = slope.astype(jnp.bfloat16)
        total[1] += jnp.dot(slope_cast, block, preferred_element_type=jnp.float32)
        total[0, where, :] += lax.dot_general(
            slope_cast, cast[1], (((0,), (0,)), ((), ())), preferred_element_type=jnp.float32
        )

    def slopes(route, slot, target):
        side = slot // parts
        values = arrived[route, slot].astype(jnp.float32)
        target[...] = (values * inverse_norm(values)).astype(jnp.bfloat16)
        cosine = lax.dot_general(
            cast[side], target[...], (((1,), (1,)), ((), ())), preferred_element_type=jnp.float32
        )
        loss, slope = loss_and_slope(scale_value * cosine + bias_value)
        note(side, loss, slope, cosine)
        return slope.astype(jnp.bfloat16)

    def meet(route, slot):
        slope_cast = slopes(route, slot, unit)
        total[slot // parts] += jnp.dot(
            slope_cast, unit[...], preferred_element_type=jnp.float32
        )

    def incoming(route, slot):
        return pltpu.make_async_remote_copy(
            src_ref=arrived.at[route, slot],
            dst_ref=arrived.at[route, slot],
            send_sem=send_sem.at[route, slot],
            recv_sem=recv_sem.at[route, slot],
            device_id=core,
            device_id_type=MESH,
        )

    def along_y(with_own, slot, carry):
        incoming(NEAR, slot).wait_recv()
        relay(slot).start()
        meet(NEAR, slot)
        if with_own:
            own(slot)
        incoming(CORE, slot).wait_recv()
        meet(CORE, slot)

        @pl.when(slot > 0)
        def _():
            incoming(FAR, slot - 1).wait_recv()
            meet(FAR, slot - 1)

        return carry

    lax.fori_loop(0, parts, functools.partial(along_y, True), 0)
    lax.fori_loop(parts, parts + 2, functools.partial(along_y, False), 0)

    @pl.when(patient)
    def _():
        send(LONG, far, 1, parts)

    lax.fori_loop(parts + 2, steps, functools.partial(along_y, False), 0)
    incoming(FAR, steps - 1).wait_recv()
    meet(FAR, steps - 1)

    def along_z(slot, carry):
        incoming(LONG, slot).wait_recv()
        meet(LONG, slot)
        return carry

    lax.fori_loop(0, parts, along_z, 0)

    def exchange(stage):
        return pltpu.make_async_remote_copy(
            src_ref=sums.at[stage],
            dst_ref=heard.at[stage],
            send_sem=sum_send.at[stage],
            recv_sem=sum_recv.at[stage],
            device_id=plane[stage],
            device_id_type=MESH,
        )

    def tell(device, index, slot):
        return pltpu.make_async_remote_copy(
            src_ref=sums.at[len(plane)],
            dst_ref=levels.at[slot],
            send_sem=level_send.at[index],
            recv_sem=level_recv.at[slot],
            device_id=device,
            device_id_type=MESH,
        )

    sums[0] = jnp.zeros_like(sums[0])
    sums[0, pl.ds(0, 3)] = jnp.sum(stats[0], axis=1)
    exchange(0).start()

    def finish_image(part, carry):
        where = pl.ds(pl.multiple_of(part * CHUNK, CHUNK), CHUNK)
        scaling = inverse[0, where, :]
        rows_unit = raw[0, where, :].astype(jnp.float32) * scaling
        total[0, where, :] = project(rows_unit, scale_value * total[0, where, :]) * scaling
        return carry

    for stage in range(len(plane)):
        exchange(stage).wait()
        sums[stage + 1] = sums[stage] + heard[stage]
        if stage + 1 < len(plane):
            exchange(stage + 1).start()

    for parity, column in enumerate(columns):

        @pl.when(narrow % 2 == parity)
        def _(parity=parity, column=column):
            for index, (device, _) in enumerate(column):
                tell(device, index, level).start()
            if parity == 0:
                levels[level] = sums[len(plane)]

    lax.fori_loop(0, parts, finish_image, 0)

    factor[...] = jnp.full(factor.shape, scale_value, jnp.float32)

    def drain(slot, carry):
        for route in (CORE, NEAR, FAR):
            incoming(route, slot).wait_send()
        return carry

    lax.fori_loop(0, steps, drain, 0)

    def along_z_sent(slot, carry):
        incoming(LONG, slot - parts).wait_send()
        return along_z(slot, carry)

    lax.fori_loop(parts, steps - 1, along_z_sent, 0)
    incoming(LONG, steps - 1).wait_recv()
    last_slope[...] = slopes(LONG, steps - 1, last_unit)

    for slot in range(parts - 1, steps):
        incoming(LONG, slot).wait_send()
    for parity, column in enumerate(columns):

        @pl.when(narrow % 2 == parity)
        def _(column=column):
            for index, (device, slot) in enumerate(column):
                tell(device, index, slot).wait_recv()
                tell(device, index, level).wait_send()

    halves = len(plane) + 1
    sums[halves] = jnp.sum(levels[...], axis=0)
    other_half = pltpu.make_async_remote_copy(
        src_ref=sums.at[halves],
        dst_ref=heard.at[len(plane)],
        send_sem=sum_send.at[len(plane)],
        recv_sem=sum_recv.at[len(plane)],
        device_id=core,
        device_id_type=MESH,
    )
    other_half.start()
    other_half.wait()
    answer[...] = sums[halves] + heard[len(plane)]


def finish_kernel(
    count,
    total,
    raw,
    inverse,
    answer,
    last_slope,
    last_unit,
    factor,
    image_out,
    text_out,
    totals_out,
    done,
    totals,
    sem,
):
    rows = total.shape[1]
    parts = rows // CHUNK
    image_copy = pltpu.make_async_copy(total.at[0], image_out, sem.at[parts])
    image_copy.start()
    scale_value = factor[0:1, 0:1]

    def store(part):
        where = pl.ds(pl.multiple_of(part * CHUNK, CHUNK), CHUNK)
        return pltpu.make_async_copy(done.at[where], text_out.at[where], sem.at[part])

    def body(part, carry):
        where = pl.ds(pl.multiple_of(part * CHUNK, CHUNK), CHUNK)
        scaling = inverse[1, where, :]
        rows_unit = raw[1, where, :].astype(jnp.float32) * scaling
        whole = total[1, where, :] + jnp.dot(
            last_slope[where, :], last_unit[...], preferred_element_type=jnp.float32
        )
        done[where, :] = project(rows_unit, scale_value * whole) * scaling
        store(part).start()
        return carry

    lax.fori_loop(0, parts, body, 0)
    for index in range(3):
        totals[index] = jnp.sum(answer[index]) / count
    totals_copy = pltpu.make_async_copy(totals, totals_out, sem.at[parts + 1])
    totals_copy.start()
    for part in range(parts):
        store(part).wait()
    image_copy.wait()
    totals_copy.wait()


def per_device(image_rows, text_rows, labels, scale, bias):
    rows, width = image_rows.shape
    parts = rows // CHUNK
    dma = pltpu.SemaphoreType.DMA
    anywhere = pl.BlockSpec(memory_space=pl.ANY)
    here = pl.BlockSpec(memory_space=pltpu.VMEM)
    products = 20 * rows * rows * width
    held = pl.pallas_call(
        functools.partial(exchange_kernel, rows),
        out_shape=(
            pltpu.VMEM((2, rows, width), jnp.float32),
            pltpu.VMEM((2, rows, width), jnp.bfloat16),
            pltpu.VMEM((2, rows, 1), jnp.float32),
            pltpu.VMEM((8, CHUNK), jnp.float32),
            pltpu.VMEM((rows, CHUNK), jnp.bfloat16),
            pltpu.VMEM((CHUNK, width), jnp.bfloat16),
            pltpu.VMEM((8, CHUNK), jnp.float32),
        ),
        in_specs=[pl.BlockSpec(memory_space=pltpu.HBM)] * 5,
        out_specs=(here,) * 7,
        scratch_shapes=[
            pltpu.VMEM((4, 2 * parts, CHUNK, width), jnp.bfloat16),
            pltpu.VMEM((2, rows, width), jnp.bfloat16),
            pltpu.VMEM((1, rows), jnp.int32),
            pltpu.SMEM((1,), jnp.float32),
            pltpu.SMEM((1,), jnp.float32),
            pltpu.VMEM((CHUNK, width), jnp.bfloat16),
            pltpu.VMEM((2, 3, 8, CHUNK), jnp.float32),
            pltpu.VMEM((7, 8, CHUNK), jnp.float32),
            pltpu.VMEM((6, 8, CHUNK), jnp.float32),
            pltpu.VMEM((8, 8, CHUNK), jnp.float32),
            dma((5,)),
            dma((4, 2 * parts)),
            dma((4, 2 * parts)),
            dma((6,)),
            dma((6,)),
            dma((4,)),
            dma((8,)),
            pltpu.SemaphoreType.REGULAR,
            pltpu.SemaphoreType.REGULAR,
            pltpu.SemaphoreType.REGULAR,
            pltpu.SemaphoreType.REGULAR,
        ],
        compiler_params=pltpu.CompilerParams(
            collective_id=0, has_side_effects=True, vmem_limit_bytes=54 << 20
        ),
        cost_estimate=pl.CostEstimate(
            flops=2 * products, bytes_accessed=8 * rows * width, transcendentals=8 * rows * rows
        ),
        name="exchange",
    )(image_rows, text_rows, labels.reshape(1, rows), scale, bias)
    gradient = jax.ShapeDtypeStruct((rows, width), jnp.float32)
    return pl.pallas_call(
        functools.partial(finish_kernel, rows * lax.axis_size(("wide", "narrow"))),
        out_shape=(gradient, gradient, jax.ShapeDtypeStruct((3,), jnp.float32)),
        in_specs=[here] * 7,
        out_specs=(anywhere,) * 3,
        scratch_shapes=[
            pltpu.VMEM((rows, width), jnp.float32),
            pltpu.SMEM((3,), jnp.float32),
            dma((parts + 2,)),
        ],
        compiler_params=pltpu.CompilerParams(vmem_limit_bytes=24 << 20),
        name="finish",
    )(*held)


def solution(mesh):
    split = P(("wide", "narrow"), None)
    return jax.shard_map(
        per_device,
        mesh=mesh,
        in_specs=(split, split, P(("wide", "narrow")), P(), P()),
        out_specs=(split, split, P()),
        check_vma=False,
    )
```
